32 devices in a mesh: fsdp: 4 (over y, core), cand: 8 (over z, x).
Axes of the slice: x: 2, y: 2, z: 4, core: 2. Of those that a mesh axis runs over, the one named last changes fastest.
Arguments:
- positions_init: float32 [256, 8192], P(('fsdp', 'cand')), may hold values from -6 to 6
- momenta_init: float32 [256, 8192], P(('fsdp', 'cand')), may hold values from -6 to 6
- kernel: bfloat16 [4096, 8192], P('fsdp'), may hold values from -0.0625 to 0.0625
- bias: bfloat16 [4096], P('fsdp'), may hold values from -4 to 4
- amplitude: bfloat16 [4096], P('fsdp'), may hold values from 0.3984375 to 2.5
- shift: float32 [8192], replicated, may hold values from -4 to 4
- omega: bfloat16 [8192, 8192], P('fsdp', 'cand'), may hold values from -0.0625 to 0.0625
- phase: float32 [8192], P('fsdp'), may hold values from -3.140625 to 3.140625
- samples: bfloat16 [8192, 128], P('fsdp'), may hold values from -6 to 6
Outputs:
- tracked: bfloat16 [256, 8192], P(('fsdp', 'cand'))
- final_positions: float32 [256, 8192], P(('fsdp', 'cand'))
- acquisition: float32 [256, 128], P(('fsdp', 'cand'))
The draws below stay inside these ranges and needn't reach their ends.
All inputs are finite; a program needn't handle non-finite values.
Results may differ from the reference program's by a relative error of at most 0.0062.
Values may be sent and summed in bfloat16 or wider, within the bound.
No kernel may reach another device: no remote copies, remote signals or barrier semaphores. Data moves between devices by JAX's collectives and lax.ppermute only.
A program may use at most 192 MiB of HBM per device.

```python
import math
import jax
import jax.numpy as jnp
from jax import lax

H = 8192
M = 4096
F = 8192
S = 128
TURNS = 1
CANDS = 256


def block_scale(key, dims, pieces, low, top_value):
    gain = 1.0
    for position, shards_of in pieces:
        steps = jax.random.uniform(jax.random.fold_in(jax.random.fold_in(key, 6), position), (shards_of,), jnp.float32, low / len(pieces), top_value / len(pieces))
        gain = gain * jnp.repeat(jnp.exp(steps), dims[position] // shards_of).reshape((-1,) + (1,) * (len(dims) - 1 - position))
    return gain


def bell_draw(stream_key, extent, width, limit, split=(), held_as=jnp.bfloat16):
    gain = block_scale(stream_key, extent, split, -0.22, 0.18) if split else 1.0
    array = jax.random.normal(stream_key, extent, jnp.float32) * width * gain
    return jnp.minimum(jnp.maximum(array, -limit), limit).astype(held_as)


def setup_inputs(seed: int = 0) -> dict:
    key_list = jax.random.split(jax.random.key(seed), 10)
    positions_init = bell_draw(key_list[0], (CANDS, H), 1.0, 6.0, ((0, 32),), jnp.float32)
    momenta_init = bell_draw(key_list[1], (CANDS, H), 1.0, 6.0, ((0, 32),), jnp.float32)
    kernel = bell_draw(key_list[2], (M, H), H ** -0.5, 0.0625, ((0, 4),))
    bias = bell_draw(key_list[3], (M,), 0.7, 4.0, ((0, 4),))
    amplitude = jnp.clip(jnp.exp(math.log(2.5) - 1.8364954 * jax.random.uniform(key_list[4], (M,), jnp.float32) ** block_scale(key_list[4], (M,), ((0, 4),), -0.2, 0.2)), 0.3984375, 2.5).astype(jnp.bfloat16)
    shift = bell_draw(key_list[5], (H,), 0.7, 4.0, (), jnp.float32)
    omega = bell_draw(key_list[6], (F, H), H ** -0.5, 0.0625, ((0, 4), (1, 8)))
    phase = jnp.clip(jax.random.uniform(key_list[7], (F,), jnp.float32, -3.140625, 3.140625), -3.140625, 3.140625)
    samples = bell_draw(key_list[8], (F, S), 1.0, 6.0, ((0, 4),))
    return dict(positions_init=positions_init, momenta_init=momenta_init, kernel=kernel, bias=bias, amplitude=amplitude, shift=shift, omega=omega, phase=phase, samples=samples)


def reference(positions_init, momenta_init, kernel, bias, amplitude, shift, omega, phase, samples):
    positions = positions_init
    momenta = momenta_init
    bias_wide = bias.astype(jnp.float32)
    amp_wide = amplitude.astype(jnp.float32)
    for turn_index in range(TURNS):
        rounded = momenta.astype(jnp.bfloat16)
        scores = lax.dot_general(rounded, kernel, (((1,), (1,)), ((), ())), preferred_element_type=jnp.float32) + bias_wide[None, :]
        activated = (amp_wide[None, :] * jnp.tanh(scores)).astype(jnp.bfloat16)
        force = jnp.dot(activated, kernel, preferred_element_type=jnp.float32)
        positions, momenta = (momenta + shift[None, :], force - positions)
    tracked = momenta.astype(jnp.bfloat16)
    angles = lax.dot_general(tracked, omega, (((1,), (1,)), ((), ())), preferred_element_type=jnp.float32)
    features = (jnp.sqrt(2.0 / F) * jnp.cos(angles + phase[None, :])).astype(jnp.bfloat16)
    acquisition = jnp.dot(features, samples, preferred_element_type=jnp.float32)
    return (tracked, positions, acquisition)
```

```python
import jax
import jax.numpy as jnp
from jax import lax
from jax.sharding import PartitionSpec as P


def local(positions_init, momenta_init, kernel, bias, amplitude, shift, omega, phase, samples):
    f32 = jnp.float32
    features_all = samples.shape[0] * lax.axis_size("fsdp")
    n_fsdp, n_cand = lax.axis_size("fsdp"), lax.axis_size("cand")
    own = positions_init.shape[0]
    rounded = lax.all_gather(momenta_init.astype(jnp.bfloat16), "fsdp", axis=0, tiled=True)
    scores = lax.dot_general(rounded, kernel, (((1,), (1,)), ((), ())), preferred_element_type=f32)
    scores = scores + bias.astype(f32)[None, :]
    activated = (amplitude.astype(f32)[None, :] * jnp.tanh(scores)).astype(jnp.bfloat16)
    partial = jnp.dot(activated, kernel, preferred_element_type=f32)
    force = lax.psum_scatter(partial, "fsdp", scatter_dimension=0, tiled=True)
    positions = momenta_init + shift[None, :]
    tracked = (force - positions_init).astype(jnp.bfloat16)
    columns = lax.all_to_all(tracked, "cand", split_axis=1, concat_axis=0, tiled=True)
    every = lax.all_gather(columns, "fsdp", axis=0, tiled=False)
    every = every.reshape(n_fsdp, n_cand, own, -1).transpose(1, 0, 2, 3).reshape(n_fsdp * n_cand * own, -1)
    part_angles = lax.dot_general(every, omega, (((1,), (1,)), ((), ())), preferred_element_type=f32)
    angles = lax.psum_scatter(part_angles, "cand", scatter_dimension=0, tiled=True)
    features = (jnp.sqrt(2.0 / features_all) * jnp.cos(angles + phase[None, :])).astype(jnp.bfloat16)
    acquisition = lax.psum_scatter(
        jnp.dot(features, samples, preferred_element_type=f32), "fsdp", scatter_dimension=0, tiled=True
    )
    return (tracked, positions, acquisition)


def solution(mesh):
    both = P(("fsdp", "cand"), None)
    return jax.shard_map(
        local,
        mesh=mesh,
        in_specs=(both, both, P("fsdp", None), P("fsdp"), P("fsdp"), P(), P("fsdp", "cand"), P("fsdp"), P("fsdp", None)),
        out_specs=(both, both, both),
        check_vma=False,
    )
```

```python
import functools
import math

import jax
import jax.numpy as jnp
from jax import lax
from jax.experimental import pallas as pl
from jax.experimental.pallas import tpu as pltpu
from jax.sharding import PartitionSpec as P

F32, BF16 = jnp.float32, jnp.bfloat16
NT = (((1,), (1,)), ((), ()))
VM = pl.BlockSpec(memory_space=pltpu.VMEM)


def swap(x, axis, bit):
    n = lax.axis_size(axis)
    return lax.ppermute(x, axis, [(i, i ^ bit) for i in range(n)])


def force_kernel(m_ref, k_ref, b_ref, a_ref, keep_ref, send_ref, act_ref, *, rows, cols):
    hidden, width = k_ref.shape
    half = keep_ref.shape[0]

    @pl.loop(0, hidden // rows)
    def _(j):
        r = pl.ds(pl.multiple_of(j * rows, rows), rows)
        s = lax.dot_general(m_ref[...], k_ref[r, :], NT, preferred_element_type=F32)
        s = s + b_ref[:, r].astype(F32)
        act_ref[:, r] = (a_ref[:, r].astype(F32) * jnp.tanh(s)).astype(BF16)

    @pl.loop(0, width // cols)
    def _(j):
        c = pl.ds(pl.multiple_of(j * cols, cols), cols)
        f = jnp.dot(act_ref[...], k_ref[:, c], preferred_element_type=F32)
        keep_ref[:, c] = f[:half]
        send_ref[:, c] = f[half:]


def force_parts(m, kernel, bias, amplitude):
    hidden, width = kernel.shape
    n = m.shape[0]
    out = jax.ShapeDtypeStruct((n // 2, width), F32)
    return pl.pallas_call(
        functools.partial(force_kernel, rows=math.gcd(hidden, 512), cols=math.gcd(width, 2048)),
        out_shape=(out, out),
        in_specs=[VM, VM, VM, VM],
        out_specs=(VM, VM),
        scratch_shapes=[pltpu.VMEM((n, hidden), BF16)],
        compiler_params=pltpu.CompilerParams(vmem_limit_bytes=34 * 2**20),
        name="force_parts",
    )(m, pltpu.with_memory_space_constraint(kernel, pltpu.VMEM), bias[None, :], amplitude[None, :])


def angle_kernel(t_ref, w_ref, keep_ref, send_ref, *, block):
    a = lax.dot_general(t_ref[...], w_ref[...], NT, preferred_element_type=F32)
    for i in range(t_ref.shape[0] // (2 * block)):
        keep_ref[i * block : (i + 1) * block, :] = a[2 * i * block : (2 * i + 1) * block]
        send_ref[i * block : (i + 1) * block, :] = a[(2 * i + 1) * block : (2 * i + 2) * block].astype(BF16)


def angle_parts(t, omega, block):
    n, feats = t.shape[0] // 2, omega.shape[0]
    cols = math.gcd(feats, 512)
    return pl.pallas_call(
        functools.partial(angle_kernel, block=block),
        grid=(feats // cols,),
        out_shape=(jax.ShapeDtypeStruct((n, feats), F32), jax.ShapeDtypeStruct((n, feats), BF16)),
        in_specs=[
            pl.BlockSpec(t.shape, lambda i: (0, 0)),
            pl.BlockSpec((cols, omega.shape[1]), lambda i: (i, 0)),
        ],
        out_specs=(pl.BlockSpec((n, cols), lambda i: (0, i)), pl.BlockSpec((n, cols), lambda i: (0, i))),
        compiler_params=pltpu.CompilerParams(vmem_limit_bytes=24 * 2**20),
        name="angle_parts",
    )(t, omega)


def local(positions_init, momenta_init, kernel, bias, amplitude, shift, omega, phase, samples):
    n_fsdp, n_cand = lax.axis_size("fsdp"), lax.axis_size("cand")
    own, width = positions_init.shape
    feats = omega.shape[0]
    bits = [1 << b for b in range(n_fsdp.bit_length() - 1)]
    cand = lax.axis_index("cand")
    outer, inner = cand // 2, cand % 2
    n_outer = n_cand // 2

    m = momenta_init.astype(BF16)
    for bit in reversed(bits):
        m = jnp.concatenate([m, swap(m, "fsdp", bit)], axis=0)
    keep, send = force_parts(m, kernel, bias, amplitude)
    keep = keep + swap(send, "fsdp", 1)
    for bit in bits[1:]:
        half = keep.shape[0] // 2
        keep = keep[:half] + swap(keep[half:].astype(BF16), "fsdp", bit).astype(F32)
    tracked = (keep - positions_init).astype(BF16)
    positions = momenta_init + shift[None, :]

    by_outer = tracked.reshape(own, n_outer, width // n_outer)
    piece = lambda j: lax.dynamic_index_in_dim(by_outer, outer ^ j, axis=1, keepdims=False)
    t = jnp.concatenate([piece(0)] + [swap(piece(j), "cand", 2 * j) for j in range(1, n_outer)], axis=0)
    lo, hi = t[:, : t.shape[1] // 2], t[:, t.shape[1] // 2 :]
    t = jnp.concatenate([jnp.where(inner == 0, lo, hi), swap(jnp.where(inner == 0, hi, lo), "cand", 1)], axis=0)
    for bit in reversed(bits):
        t = jnp.concatenate([t, swap(t, "fsdp", bit)], axis=0)

    keep, send = angle_parts(t, omega, n_outer * own)
    keep = keep + swap(send, "cand", 1).astype(F32)
    keep = keep.reshape(n_fsdp, n_outer, own, feats)
    angles = keep[:, 0]
    for j in range(1, n_outer):
        angles = angles + swap(keep[:, j].astype(BF16), "cand", 2 * j).astype(F32)
    angles = angles.reshape(n_fsdp * own, feats)
    features = (jnp.sqrt(2.0 / (feats * n_fsdp)) * jnp.cos(angles + phase[None, :])).astype(BF16)
    acquisition = jnp.dot(features, samples, preferred_element_type=F32)
    for bit in bits:
        half = acquisition.shape[0] // 2
        acquisition = acquisition[:half] + swap(acquisition[half:], "fsdp", bit)
    return (tracked, positions, acquisition)


def solution(mesh):
    both = P(("fsdp", "cand"), None)
    return jax.shard_map(
        local,
        mesh=mesh,
        in_specs=(both, both, P("fsdp", None), P("fsdp"), P("fsdp"), P(), P("fsdp", "cand"), P("fsdp"), P("fsdp", None)),
        out_specs=(both, both, both),
        check_vma=False,
    )
```

```python
import functools
import math

import jax
import jax.numpy as jnp
from jax import lax
from jax.experimental import pallas as pl
from jax.experimental.pallas import tpu as pltpu
from jax.sharding import PartitionSpec as P

F32, BF16 = jnp.float32, jnp.bfloat16
NT = (((1,), (1,)), ((), ()))
VM = pl.BlockSpec(memory_space=pltpu.VMEM)


def swap(x, axis, bit):
    n = lax.axis_size(axis)
    return lax.ppermute(x, axis, [(i, i ^ bit) for i in range(n)])


def swap_both(x, fsdp_bit, cand_bit):
    m, n = lax.axis_size("fsdp"), lax.axis_size("cand")
    pairs = [(i * n + j, (i ^ fsdp_bit) * n + (j ^ cand_bit)) for i in range(m) for j in range(n)]
    return lax.ppermute(x, ("fsdp", "cand"), pairs)


def load_kernel(src_ref, *refs, start):
    *dst_refs, sems = refs
    copies = []
    for dst_ref in dst_refs:
        copies.append(pltpu.make_async_copy(src_ref.at[pl.ds(start, dst_ref.shape[0])], dst_ref, sems.at[len(copies)]))
        copies[-1].start()
        start += dst_ref.shape[0]
    for c in copies:
        c.wait()


def load(x, start, sizes, name):
    return pl.pallas_call(
        functools.partial(load_kernel, start=start),
        out_shape=tuple(pltpu.VMEM((rows, x.shape[1]), x.dtype) for rows in sizes),
        in_specs=[pl.BlockSpec(memory_space=pltpu.HBM)],
        out_specs=(VM,) * len(sizes),
        scratch_shapes=[pltpu.SemaphoreType.DMA((len(sizes),))],
        compiler_params=pltpu.CompilerParams(vmem_limit_bytes=2**20),
        cost_estimate=pl.CostEstimate(
            flops=0, bytes_accessed=2 * sum(sizes) * x.shape[1] * x.dtype.itemsize, transcendentals=0
        ),
        name=name,
    )(x)


def force_kernel(m_ref, first_ref, second_ref, b_ref, a_ref, keep_ref, send_ref, act_ref, *, cols):
    early, width = first_ref.shape
    half = keep_ref.shape[0]
    at = 0
    for ref in (first_ref, second_ref):
        s = lax.dot_general(m_ref[...], ref[...], NT, preferred_element_type=F32)
        c = slice(at, at + ref.shape[0])
        s = s + b_ref[:, c].astype(F32)
        act_ref[:, c] = (a_ref[:, c].astype(F32) * jnp.tanh(s)).astype(BF16)
        at += ref.shape[0]

    @pl.loop(0, width // cols)
    def _(j):
        c = pl.ds(pl.multiple_of(j * cols, cols), cols)
        f = jnp.dot(act_ref[:, :early], first_ref[:, c], preferred_element_type=F32)
        f = f + jnp.dot(act_ref[:, early:], second_ref[:, c], preferred_element_type=F32)
        keep_ref[:, c] = f[:half]
        send_ref[:, c] = f[half:]


def force_parts(m, first, second, bias, amplitude):
    n, width = m.shape
    hidden = bias.shape[0]
    out = pltpu.VMEM((n // 2, width), F32)
    return pl.pallas_call(
        functools.partial(force_kernel, cols=math.gcd(width, 2048)),
        out_shape=(out, out),
        in_specs=[VM] * 5,
        out_specs=(VM, VM),
        scratch_shapes=[pltpu.VMEM((n, hidden), BF16)],
        compiler_params=pltpu.CompilerParams(vmem_limit_bytes=8 * 2**20),
        cost_estimate=pl.CostEstimate(
            flops=4 * 256 * hidden * width, bytes_accessed=2 * hidden * width, transcendentals=n * hidden
        ),
        name="force_parts",
    )(m, first, second, bias[None, :], amplitude[None, :])


def angle_kernel(t_ref, w_ref, keep_ref, send_ref, *, block):
    a = lax.dot_general(t_ref[...], w_ref[...], NT, preferred_element_type=F32)
    for i in range(t_ref.shape[0] // (2 * block)):
        keep_ref[i * block : (i + 1) * block, :] = a[2 * i * block : (2 * i + 1) * block]
        send_ref[i * block : (i + 1) * block, :] = a[(2 * i + 1) * block : (2 * i + 2) * block].astype(BF16)


def angle_parts(t, omega, block):
    n, cols = t.shape[0] // 2, omega.shape[0]
    return pl.pallas_call(
        functools.partial(angle_kernel, block=block),
        out_shape=(pltpu.VMEM((n, cols), F32), pltpu.VMEM((n, cols), BF16)),
        in_specs=[VM, VM],
        out_specs=(VM, VM),
        compiler_params=pltpu.CompilerParams(vmem_limit_bytes=8 * 2**20),
        cost_estimate=pl.CostEstimate(
            flops=4 * n * cols * t.shape[1], bytes_accessed=2 * cols * t.shape[1], transcendentals=0
        ),
        name="angle_parts",
    )(t, omega)


def local(positions_init, momenta_init, kernel, bias, amplitude, shift, omega, phase, samples):
    n_fsdp, n_cand = lax.axis_size("fsdp"), lax.axis_size("cand")
    own, width = positions_init.shape
    feats = omega.shape[0]
    bits = [1 << b for b in range(n_fsdp.bit_length() - 1)]
    cand = lax.axis_index("cand")
    outer, inner = cand // 2, cand % 2
    n_outer = n_cand // 2
    kernel = pltpu.with_memory_space_constraint(kernel, pltpu.HBM)
    omega = pltpu.with_memory_space_constraint(omega, pltpu.HBM)

    early = kernel.shape[0] * 5 // 8
    first = load(kernel, 0, [early], "load_first")[0]
    second = load(kernel, early, [kernel.shape[0] - early], "load_second")[0]
    m = momenta_init.astype(BF16)
    for bit in reversed(bits):
        if bit == 1:
            m, first = lax.optimization_barrier((m, first))
        m = jnp.concatenate([m, swap(m, "fsdp", bit)], axis=0)
    keep, send = force_parts(m, first, second, bias, amplitude)
    keep = keep + swap(send, "fsdp", 1)
    for bit in bits[1:]:
        half = keep.shape[0] // 2
        keep = keep[:half] + swap(keep[half:].astype(BF16), "fsdp", bit).astype(F32)
    tracked = (keep - positions_init).astype(BF16)

    by_outer = tracked.reshape(own, n_outer, width // n_outer)
    piece = lambda j: lax.dynamic_index_in_dim(by_outer, outer ^ j, axis=1, keepdims=False)
    t = jnp.concatenate([piece(0)] + [swap(piece(j), "cand", 2 * j) for j in range(1, n_outer)], axis=0)
    lo, hi = t[:, : t.shape[1] // 2], t[:, t.shape[1] // 2 :]
    mine, other = jnp.where(inner == 0, lo, hi), jnp.where(inner == 0, hi, lo)
    mine, other, omega = lax.optimization_barrier((mine, other, omega))
    omega = load(omega, 0, [feats // 2, feats // 2], "load_omega")
    t = jnp.concatenate([mine, swap(other, "cand", 1), swap(mine, "fsdp", 2), swap_both(other, 2, 1)], axis=0)
    t, omega = lax.optimization_barrier((t, omega))
    for bit in reversed(bits):
        if bit == 2:
            continue
        t = jnp.concatenate([t, swap(t, "fsdp", bit)], axis=0)
    t, momenta_init = lax.optimization_barrier((t, momenta_init))
    positions = momenta_init + shift[None, :]

    sums = []
    for w in omega:
        keep, send = angle_parts(t, w, n_outer * own)
        sums.append(keep + swap(send, "cand", 1).astype(F32))
    acquisition = 0.0
    start = 0
    for keep in sums:
        cols = keep.shape[1]
        keep = keep.reshape(n_fsdp, n_outer, own, cols)
        angles = keep[:, 0]
        for j in range(1, n_outer):
            angles = angles + swap(keep[:, j].astype(BF16), "cand", 2 * j).astype(F32)
        c = slice(start, start + cols)
        start += cols
        angles = angles.reshape(n_fsdp * own, cols) + phase[None, c]
        features = (jnp.sqrt(2.0 / (feats * n_fsdp)) * jnp.cos(angles)).astype(BF16)
        acquisition = acquisition + jnp.dot(features, samples[c], preferred_element_type=F32)
    for bit in bits:
        half = acquisition.shape[0] // 2
        acquisition = acquisition[:half] + swap(acquisition[half:], "fsdp", bit)
    return (tracked, positions, acquisition)


def solution(mesh):
    both = P(("fsdp", "cand"), None)
    return jax.shard_map(
        local,
        mesh=mesh,
        in_specs=(both, both, P("fsdp", None), P("fsdp"), P("fsdp"), P(), P("fsdp", "cand"), P("fsdp"), P("fsdp", None)),
        out_specs=(both, both, both),
        check_vma=False,
    )
```

```python
import functools
import math

import jax
import jax.numpy as jnp
from jax import lax
from jax.experimental import pallas as pl
from jax.experimental.pallas import tpu as pltpu
from jax.sharding import PartitionSpec as P

F32, BF16 = jnp.float32, jnp.bfloat16
NT = (((1,), (1,)), ((), ()))
VM = pl.BlockSpec(memory_space=pltpu.VMEM)


def swap(x, axis, bit):
    n = lax.axis_size(axis)
    return lax.ppermute(x, axis, [(i, i ^ bit) for i in range(n)])


def swap_both(x, fsdp_bit, cand_bit):
    m, n = lax.axis_size("fsdp"), lax.axis_size("cand")
    pairs = [(i * n + j, (i ^ fsdp_bit) * n + (j ^ cand_bit)) for i in range(m) for j in range(n)]
    return lax.ppermute(x, ("fsdp", "cand"), pairs)


def round_kernel(x_ref, out_ref):
    out_ref[...] = x_ref[...].astype(BF16)


def rounded(x):
    return pl.pallas_call(
        round_kernel,
        out_shape=pltpu.VMEM(x.shape, BF16),
        in_specs=[VM],
        out_specs=VM,
        compiler_params=pltpu.CompilerParams(vmem_limit_bytes=2**20),
        cost_estimate=pl.CostEstimate(flops=10**10, bytes_accessed=6 * x.size, transcendentals=0),
        name="rounded",
    )(x)


def load_kernel(src_ref, *refs, start):
    *dst_refs, sems = refs
    copies = []
    for dst_ref in dst_refs:
        copies.append(pltpu.make_async_copy(src_ref.at[pl.ds(start, dst_ref.shape[0])], dst_ref, sems.at[len(copies)]))
        copies[-1].start()
        start += dst_ref.shape[0]
    for c in copies:
        c.wait()


def load(x, start, sizes, name):
    return pl.pallas_call(
        functools.partial(load_kernel, start=start),
        out_shape=tuple(pltpu.VMEM((rows, x.shape[1]), x.dtype) for rows in sizes),
        in_specs=[pl.BlockSpec(memory_space=pltpu.HBM)],
        out_specs=(VM,) * len(sizes),
        scratch_shapes=[pltpu.SemaphoreType.DMA((len(sizes),))],
        compiler_params=pltpu.CompilerParams(vmem_limit_bytes=2**20),
        cost_estimate=pl.CostEstimate(
            flops=0, bytes_accessed=2 * sum(sizes) * x.shape[1] * x.dtype.itemsize, transcendentals=0
        ),
        name=name,
    )(x)


def force_kernel(m_ref, k_ref, b_ref, a_ref, keep_ref, send_ref, act_ref):
    hidden = k_ref.shape[0]
    rows = math.gcd(hidden, 512)
    for at in range(0, hidden, rows):
        c = slice(at, at + rows)
        s = lax.dot_general(m_ref[...], k_ref[c, :], NT, preferred_element_type=F32)
        s = s + b_ref[:, c].astype(F32)
        act_ref[:, c] = (a_ref[:, c].astype(F32) * jnp.tanh(s)).astype(BF16)
    columns_kernel(act_ref, k_ref, keep_ref, send_ref, start=0)


def columns_kernel(act_ref, k_ref, keep_ref, send_ref, *, start):
    half, width = keep_ref.shape
    step = math.gcd(width, 2048)

    @pl.loop(0, width // step)
    def _(j):
        c = pl.ds(pl.multiple_of(start + j * step, step), step)
        f = jnp.dot(act_ref[...], k_ref[:, c], preferred_element_type=F32)
        c = pl.ds(pl.multiple_of(j * step, step), step)
        keep_ref[:, c] = f[:half]
        send_ref[:, c] = f[half:]


def force_parts(m, kernel, bias, amplitude):
    n, width = m.shape
    hidden = bias.shape[0]
    cols = width // 2
    out = pltpu.VMEM((n // 2, cols), F32)
    keep, send, act = pl.pallas_call(
        force_kernel,
        out_shape=(out, out, pltpu.VMEM((n, hidden), BF16)),
        in_specs=[VM] * 4,
        out_specs=(VM,) * 3,
        compiler_params=pltpu.CompilerParams(vmem_limit_bytes=8 * 2**20),
        cost_estimate=pl.CostEstimate(
            flops=3 * 256 * hidden * width, bytes_accessed=2 * hidden * width, transcendentals=n * hidden
        ),
        name="force_left",
    )(m, kernel, bias[None, :], amplitude[None, :])
    left = (keep, send)
    right = pl.pallas_call(
        functools.partial(columns_kernel, start=cols),
        out_shape=(out, out),
        in_specs=[VM] * 2,
        out_specs=(VM,) * 2,
        compiler_params=pltpu.CompilerParams(vmem_limit_bytes=8 * 2**20),
        cost_estimate=pl.CostEstimate(
            flops=256 * hidden * width, bytes_accessed=hidden * width, transcendentals=0
        ),
        name="force_right",
    )(act, kernel)
    return left, right


def angle_kernel(t_ref, w_ref, *out_refs, rows, starts):
    a = lax.dot_general(t_ref[...], w_ref[...], NT, preferred_element_type=F32)
    for ref, firsts in zip(out_refs, starts):
        ref[...] = jnp.concatenate([a[i : i + rows] for i in firsts], axis=0).astype(ref.dtype)


def angle_parts(t, omega, rows, outs):
    cols = omega.shape[0]
    return pl.pallas_call(
        functools.partial(angle_kernel, rows=rows, starts=[starts for _, starts in outs]),
        out_shape=tuple(pltpu.VMEM((rows * len(starts), cols), dtype) for dtype, starts in outs),
        in_specs=[VM, VM],
        out_specs=(VM,) * len(outs),
        compiler_params=pltpu.CompilerParams(vmem_limit_bytes=8 * 2**20),
        cost_estimate=pl.CostEstimate(
            flops=2 * t.shape[0] * cols * t.shape[1], bytes_accessed=2 * cols * t.shape[1], transcendentals=0
        ),
        name="angle_parts",
    )(t, omega)


def local(positions_init, momenta_init, kernel, bias, amplitude, shift, omega, phase, samples):
    n_fsdp, n_cand = lax.axis_size("fsdp"), lax.axis_size("cand")
    own, width = positions_init.shape
    feats = omega.shape[0]
    bits = [1 << b for b in range(n_fsdp.bit_length() - 1)]
    cand = lax.axis_index("cand")
    outer, inner = cand // 2, cand % 2
    n_outer = n_cand // 2
    kernel = pltpu.with_memory_space_constraint(kernel, pltpu.VMEM)
    omega = pltpu.with_memory_space_constraint(omega, pltpu.HBM)

    m = rounded(momenta_init)
    for bit in reversed(bits):
        m = jnp.concatenate([m, swap(m, "fsdp", bit)], axis=0)
    (keep, send), right = force_parts(m, kernel, bias, amplitude)
    got, right = lax.optimization_barrier((swap(send, "fsdp", 1), right))
    columns = [keep + got, right[0] + swap(right[1], "fsdp", 1)]
    for bit in bits[1:]:
        half = columns[0].shape[0] // 2
        columns = [c[:half] + swap(c[half:].astype(BF16), "fsdp", bit).astype(F32) for c in columns]
    keep = jnp.concatenate(columns, axis=1)
    tracked = (keep - positions_init).astype(BF16)

    by_outer = tracked.reshape(own, n_outer, width // n_outer)
    piece = lambda j: lax.dynamic_index_in_dim(by_outer, outer ^ j, axis=1, keepdims=False)
    t = jnp.concatenate([piece(0)] + [swap(piece(j), "cand", 2 * j) for j in range(1, n_outer)], axis=0)
    lo, hi = t[:, : t.shape[1] // 2], t[:, t.shape[1] // 2 :]
    mine, other = jnp.where(inner == 0, lo, hi), jnp.where(inner == 0, hi, lo)
    mine, other, omega = lax.optimization_barrier((mine, other, omega))
    omega = load(omega, 0, [feats * 1 // 2, feats * 1 // 2], "load_omega")
    t = jnp.concatenate([mine, swap(other, "cand", 1), swap(mine, "fsdp", 2), swap_both(other, 2, 1)], axis=0)
    t, omega = lax.optimization_barrier((t, omega))
    for bit in reversed(bits):
        if bit == 2:
            continue
        t = jnp.concatenate([t, swap(t, "fsdp", bit)], axis=0)
    t, momenta_init = lax.optimization_barrier((t, momenta_init))
    positions = momenta_init + shift[None, :]

    row = lambda f, x, z: ((f * 2 + x) * n_outer + z) * own
    by_inner = [[row(f, x, z) for z in range(n_outer) for f in range(n_fsdp)] for x in range(2)]
    group = n_fsdp * own
    outs = [(F32, by_inner[0]), (BF16, by_inner[1])]
    sums = [angle_parts(t, omega[0], own, outs), angle_parts(t, omega[1], own, outs)]
    sums = [(keep, swap(send, "cand", 1)) for keep, send in sums]
    both, ahead = [], None
    for keep, got in sums:
        keep = keep + got.astype(F32)
        blocks = [keep[j * group : (j + 1) * group] for j in range(n_outer)]
        gots = {j: swap(blocks[j].astype(BF16), "cand", 2 * j) for j in reversed(range(1, n_outer))}
        angles = blocks[0]
        for x in gots.values():
            angles = angles + x.astype(F32)
        both.append(angles)
    acquisition, start = 0.0, 0
    for angles in both:
        c = slice(start, start + angles.shape[1])
        start += angles.shape[1]
        features = (jnp.sqrt(2.0 / (feats * n_fsdp)) * jnp.cos(angles + phase[None, c])).astype(BF16)
        acquisition = acquisition + jnp.dot(features, samples[c], preferred_element_type=F32)
    parts = acquisition.reshape(2, n_fsdp // 4, 2, own, samples.shape[1])
    for bit in bits[2:]:
        half = parts.shape[1] // 2
        parts = parts[:, :half] + swap(parts[:, half:], "fsdp", bit)
    parts = parts.reshape(4, own, samples.shape[1])
    acquisition = swap(parts[3], "fsdp", 3) + swap(parts[1], "fsdp", 2) + swap(parts[2], "fsdp", 1) + parts[0]
    return (tracked, positions, acquisition)


def solution(mesh):
    both = P(("fsdp", "cand"), None)
    return jax.shard_map(
        local,
        mesh=mesh,
        in_specs=(both, both, P("fsdp", None), P("fsdp"), P("fsdp"), P(), P("fsdp", "cand"), P("fsdp"), P("fsdp", None)),
        out_specs=(both, both, both),
        check_vma=False,
    )
```

```python
import functools
import math

import jax
import jax.numpy as jnp
from jax import lax
from jax.experimental import pallas as pl
from jax.experimental.pallas import tpu as pltpu
from jax.sharding import PartitionSpec as P

F32, BF16 = jnp.float32, jnp.bfloat16
NT = (((1,), (1,)), ((), ()))
VM = pl.BlockSpec(memory_space=pltpu.VMEM)


def swap(x, axis, bit):
    n = lax.axis_size(axis)
    return lax.ppermute(x, axis, [(i, i ^ bit) for i in range(n)])


def swap_both(x, fsdp_bit, cand_bit):
    m, n = lax.axis_size("fsdp"), lax.axis_size("cand")
    pairs = [(i * n + j, (i ^ fsdp_bit) * n + (j ^ cand_bit)) for i in range(m) for j in range(n)]
    return lax.ppermute(x, ("fsdp", "cand"), pairs)


def round_kernel(x_ref, out_ref):
    out_ref[...] = x_ref[...].astype(BF16)


def rounded(x):
    return pl.pallas_call(
        round_kernel,
        out_shape=pltpu.VMEM(x.shape, BF16),
        in_specs=[VM],
        out_specs=VM,
        compiler_params=pltpu.CompilerParams(vmem_limit_bytes=2**20),
        cost_estimate=pl.CostEstimate(flops=10**10, bytes_accessed=6 * x.size, transcendentals=0),
        name="rounded",
    )(x)


def load_kernel(src_ref, *refs, start):
    *dst_refs, sems = refs
    copies = []
    for dst_ref in dst_refs:
        copies.append(pltpu.make_async_copy(src_ref.at[pl.ds(start, dst_ref.shape[0])], dst_ref, sems.at[len(copies)]))
        copies[-1].start()
        start += dst_ref.shape[0]
    for c in copies:
        c.wait()


def load(x, start, sizes, name):
    return pl.pallas_call(
        functools.partial(load_kernel, start=start),
        out_shape=tuple(pltpu.VMEM((rows, x.shape[1]), x.dtype) for rows in sizes),
        in_specs=[pl.BlockSpec(memory_space=pltpu.HBM)],
        out_specs=(VM,) * len(sizes),
        scratch_shapes=[pltpu.SemaphoreType.DMA((len(sizes),))],
        compiler_params=pltpu.CompilerParams(vmem_limit_bytes=2**20),
        cost_estimate=pl.CostEstimate(
            flops=0, bytes_accessed=2 * sum(sizes) * x.shape[1] * x.dtype.itemsize, transcendentals=0
        ),
        name=name,
    )(x)


def force_kernel(m_ref, k_ref, b_ref, a_ref, keep_ref, send_ref, act_ref):
    hidden = k_ref.shape[0]
    rows = math.gcd(hidden, 512)
    for at in range(0, hidden, rows):
        c = slice(at, at + rows)
        s = lax.dot_general(k_ref[c, :], m_ref[...], NT, preferred_element_type=F32).T
        s = s + b_ref[:, c].astype(F32)
        act_ref[:, c] = (a_ref[:, c].astype(F32) * jnp.tanh(s)).astype(BF16)
    columns_kernel(act_ref, k_ref, keep_ref, send_ref, start=0)


def columns_kernel(act_ref, k_ref, keep_ref, send_ref, *, start):
    half, width = keep_ref.shape
    step = math.gcd(width, 4096)

    @pl.loop(0, width // step)
    def _(j):
        c = pl.ds(pl.multiple_of(start + j * step, step), step)
        f = jnp.dot(act_ref[...], k_ref[:, c], preferred_element_type=F32)
        c = pl.ds(pl.multiple_of(j * step, step), step)
        keep_ref[:, c] = f[:half]
        send_ref[:, c] = f[half:]


def force_parts(m, kernel, bias, amplitude):
    n, width = m.shape
    hidden = bias.shape[0]
    cols = width // 2
    out = pltpu.VMEM((n // 2, cols), F32)
    keep, send, act = pl.pallas_call(
        force_kernel,
        out_shape=(out, out, pltpu.VMEM((n, hidden), BF16)),
        in_specs=[VM] * 4,
        out_specs=(VM,) * 3,
        compiler_params=pltpu.CompilerParams(vmem_limit_bytes=8 * 2**20),
        cost_estimate=pl.CostEstimate(
            flops=3 * 256 * hidden * width, bytes_accessed=2 * hidden * width, transcendentals=n * hidden
        ),
        name="force_left",
    )(m, kernel, bias[None, :], amplitude[None, :])
    left = (keep, send)
    right = pl.pallas_call(
        functools.partial(columns_kernel, start=cols),
        out_shape=(out, out),
        in_specs=[VM] * 2,
        out_specs=(VM,) * 2,
        compiler_params=pltpu.CompilerParams(vmem_limit_bytes=8 * 2**20),
        cost_estimate=pl.CostEstimate(
            flops=256 * hidden * width, bytes_accessed=hidden * width, transcendentals=0
        ),
        name="force_right",
    )(act, kernel)
    return left, right


def angle_kernel(t_ref, w_ref, *out_refs, rows, starts):
    a = lax.dot_general(w_ref[...], t_ref[...], NT, preferred_element_type=F32).T
    for ref, firsts in zip(out_refs, starts):
        ref[...] = jnp.concatenate([a[i : i + rows] for i in firsts], axis=0).astype(ref.dtype)


def angle_parts(t, omega, rows, outs, weight=1):
    cols = omega.shape[0]
    return pl.pallas_call(
        functools.partial(angle_kernel, rows=rows, starts=[starts for _, starts in outs]),
        out_shape=tuple(pltpu.VMEM((rows * len(starts), cols), dtype) for dtype, starts in outs),
        in_specs=[VM, VM],
        out_specs=(VM,) * len(outs),
        compiler_params=pltpu.CompilerParams(vmem_limit_bytes=8 * 2**20),
        cost_estimate=pl.CostEstimate(
            flops=weight * 2 * t.shape[0] * cols * t.shape[1], bytes_accessed=weight * 2 * cols * t.shape[1], transcendentals=0
        ),
        name="angle_parts",
    )(t, omega)


def local(positions_init, momenta_init, kernel, bias, amplitude, shift, omega, phase, samples):
    n_fsdp, n_cand = lax.axis_size("fsdp"), lax.axis_size("cand")
    own, width = positions_init.shape
    feats = omega.shape[0]
    bits = [1 << b for b in range(n_fsdp.bit_length() - 1)]
    cand = lax.axis_index("cand")
    outer, inner = cand // 2, cand % 2
    n_outer = n_cand // 2
    kernel = pltpu.with_memory_space_constraint(kernel, pltpu.VMEM)
    omega = pltpu.with_memory_space_constraint(omega, pltpu.HBM)

    m = rounded(momenta_init)
    for bit in reversed(bits):
        m = jnp.concatenate([m, swap(m, "fsdp", bit)], axis=0)
    (keep, send), right = force_parts(m, kernel, bias, amplitude)
    got, right = lax.optimization_barrier((swap(send, "fsdp", 1), right))
    columns = [keep + got, right[0] + swap(right[1], "fsdp", 1)]
    for bit in bits[1:]:
        half = columns[0].shape[0] // 2
        columns = [c[:half] + swap(c[half:].astype(BF16), "fsdp", bit).astype(F32) for c in columns]
    keep = jnp.concatenate(columns, axis=1)
    tracked = (keep - positions_init).astype(BF16)

    by_outer = tracked.reshape(own, n_outer, width // n_outer)
    piece = lambda j: lax.dynamic_index_in_dim(by_outer, outer ^ j, axis=1, keepdims=False)
    t = jnp.concatenate([piece(0)] + [swap(piece(j), "cand", 2 * j) for j in range(1, n_outer)], axis=0)
    lo, hi = t[:, : t.shape[1] // 2], t[:, t.shape[1] // 2 :]
    mine, other = jnp.where(inner == 0, lo, hi), jnp.where(inner == 0, hi, lo)
    mine, other, omega = lax.optimization_barrier((mine, other, omega))
    omega = load(omega, 0, [feats], "load_omega")[0]
    t = jnp.concatenate([mine, swap(other, "cand", 1), swap(mine, "fsdp", 2), swap_both(other, 2, 1)], axis=0)
    for bit in reversed(bits[2:]):
        t = jnp.concatenate([t, swap(t, "fsdp", bit)], axis=0)
    t, momenta_init = lax.optimization_barrier((t, momenta_init))
    positions = momenta_init + shift[None, :]

    n_rows = n_fsdp // 2 * own
    row = lambda f, x, z: ((f * 2 + x) * n_outer + z) * own
    by_inner = [[row(f, x, z) for z in range(n_outer) for f in range(n_fsdp // 2)] for x in range(2)]
    outs = [(F32, by_inner[0]), (BF16, by_inner[1])]
    keep, send = angle_parts(t, omega, own, outs)
    t, send = lax.optimization_barrier((t, send))
    sums = [(keep, swap(send, "cand", 1))]
    keep, send = angle_parts(
        jnp.concatenate([swap(t[:, : t.shape[1] // 2], "fsdp", 1), swap(t[:, t.shape[1] // 2 :], "fsdp", 1)], axis=1), omega, own, outs, 0
    )
    sums.append((keep, swap(send, "cand", 1)))
    parts = []
    for keep, got in sums:
        keep = keep + got.astype(F32)
        blocks = [keep[j * n_rows : (j + 1) * n_rows] for j in range(n_outer)]
        gots = [swap(blocks[j].astype(BF16), "cand", 2 * j) for j in reversed(range(1, n_outer))]
        angles = blocks[0] + phase[None, :]
        for x in gots:
            angles = angles + x.astype(F32)
        features = (jnp.sqrt(2.0 / (feats * n_fsdp)) * jnp.cos(angles)).astype(BF16)
        part = jnp.dot(features, samples, preferred_element_type=F32).reshape(-1, own, samples.shape[1])
        for bit in bits[2:]:
            half = part.shape[0] // 2
            part = part[:half] + swap(part[half:], "fsdp", bit)
        parts.append(part)
    mine, mates = parts
    acquisition = mine[0] + swap(mine[1], "fsdp", 2) + swap(mates[1], "fsdp", 3) + swap(mates[0], "fsdp", 1)
    return (tracked, positions, acquisition)


def solution(mesh):
    both = P(("fsdp", "cand"), None)
    return jax.shard_map(
        local,
        mesh=mesh,
        in_specs=(both, both, P("fsdp", None), P("fsdp"), P("fsdp"), P(), P("fsdp", "cand"), P("fsdp"), P("fsdp", None)),
        out_specs=(both, both, both),
        check_vma=False,
    )
```

```python
import functools
import math

import jax
import jax.numpy as jnp
from jax import lax
from jax.experimental import pallas as pl
from jax.experimental.pallas import tpu as pltpu
from jax.sharding import PartitionSpec as P

F32, BF16 = jnp.float32, jnp.bfloat16
NT = (((1,), (1,)), ((), ()))
VM = pl.BlockSpec(memory_space=pltpu.VMEM)


def swap(x, axis, bit):
    n = lax.axis_size(axis)
    return lax.ppermute(x, axis, [(i, i ^ bit) for i in range(n)])


def swap_both(x, fsdp_bit, cand_bit):
    m, n = lax.axis_size("fsdp"), lax.axis_size("cand")
    pairs = [(i * n + j, (i ^ fsdp_bit) * n + (j ^ cand_bit)) for i in range(m) for j in range(n)]
    return lax.ppermute(x, ("fsdp", "cand"), pairs)


def round_kernel(x_ref, out_ref):
    out_ref[...] = x_ref[...].astype(BF16)


def rounded(x):
    return pl.pallas_call(
        round_kernel,
        out_shape=pltpu.VMEM(x.shape, BF16),
        in_specs=[VM],
        out_specs=VM,
        compiler_params=pltpu.CompilerParams(vmem_limit_bytes=2**20),
        cost_estimate=pl.CostEstimate(flops=10**10, bytes_accessed=6 * x.size, transcendentals=0),
        name="rounded",
    )(x)


def load_kernel(src_ref, *refs, start):
    *dst_refs, sems = refs
    copies = []
    for dst_ref in dst_refs:
        copies.append(pltpu.make_async_copy(src_ref.at[pl.ds(start, dst_ref.shape[0])], dst_ref, sems.at[len(copies)]))
        copies[-1].start()
        start += dst_ref.shape[0]
    for c in copies:
        c.wait()


def load(x, start, sizes, name):
    return pl.pallas_call(
        functools.partial(load_kernel, start=start),
        out_shape=tuple(pltpu.VMEM((rows, x.shape[1]), x.dtype) for rows in sizes),
        in_specs=[pl.BlockSpec(memory_space=pltpu.HBM)],
        out_specs=(VM,) * len(sizes),
        scratch_shapes=[pltpu.SemaphoreType.DMA((len(sizes),))],
        compiler_params=pltpu.CompilerParams(vmem_limit_bytes=2**20),
        cost_estimate=pl.CostEstimate(
            flops=0, bytes_accessed=2 * sum(sizes) * x.shape[1] * x.dtype.itemsize, transcendentals=0
        ),
        name=name,
    )(x)


def force_kernel(m_ref, k_ref, b_ref, a_ref, keep_ref, send_ref, act_ref):
    hidden = k_ref.shape[0]
    rows = math.gcd(hidden, 512)
    for at in range(0, hidden, rows):
        c = slice(at, at + rows)
        s = lax.dot_general(k_ref[c, :], m_ref[...], NT, preferred_element_type=F32).T
        s = s + b_ref[:, c].astype(F32)
        act_ref[:, c] = (a_ref[:, c].astype(F32) * jnp.tanh(s)).astype(BF16)
    columns_kernel(act_ref, k_ref, keep_ref, send_ref, start=0)


def columns_kernel(act_ref, k_ref, keep_ref, send_ref, *, start):
    half, width = keep_ref.shape
    step = math.gcd(width, 4096)

    @pl.loop(0, width // step)
    def _(j):
        c = pl.ds(pl.multiple_of(start + j * step, step), step)
        f = jnp.dot(act_ref[...], k_ref[:, c], preferred_element_type=F32)
        c = pl.ds(pl.multiple_of(j * step, step), step)
        keep_ref[:, c] = f[:half]
        send_ref[:, c] = f[half:]


def force_parts(m, kernel, bias, amplitude):
    n, width = m.shape
    hidden = bias.shape[0]
    cols = width // 2
    out = pltpu.VMEM((n // 2, cols), F32)
    keep, send, act = pl.pallas_call(
        force_kernel,
        out_shape=(out, out, pltpu.VMEM((n, hidden), BF16)),
        in_specs=[VM] * 4,
        out_specs=(VM,) * 3,
        compiler_params=pltpu.CompilerParams(vmem_limit_bytes=8 * 2**20),
        cost_estimate=pl.CostEstimate(
            flops=3 * 256 * hidden * width, bytes_accessed=2 * hidden * width, transcendentals=n * hidden
        ),
        name="force_left",
    )(m, kernel, bias[None, :], amplitude[None, :])
    left = (keep, send)
    right = pl.pallas_call(
        functools.partial(columns_kernel, start=cols),
        out_shape=(out, out),
        in_specs=[VM] * 2,
        out_specs=(VM,) * 2,
        compiler_params=pltpu.CompilerParams(vmem_limit_bytes=8 * 2**20),
        cost_estimate=pl.CostEstimate(
            flops=256 * hidden * width, bytes_accessed=hidden * width, transcendentals=0
        ),
        name="force_right",
    )(act, kernel)
    return left, right


def angle_kernel(t_ref, w_ref, *out_refs, rows, starts):
    a = lax.dot_general(w_ref[...], t_ref[...], NT, preferred_element_type=F32).T
    for ref, firsts in zip(out_refs, starts):
        ref[...] = jnp.concatenate([a[i : i + rows] for i in firsts], axis=0).astype(ref.dtype)


def angle_parts(t, omega, rows, outs, weight=1):
    cols = omega.shape[0]
    return pl.pallas_call(
        functools.partial(angle_kernel, rows=rows, starts=[starts for _, starts in outs]),
        out_shape=tuple(pltpu.VMEM((rows * len(starts), cols), dtype) for dtype, starts in outs),
        in_specs=[VM, VM],
        out_specs=(VM,) * len(outs),
        compiler_params=pltpu.CompilerParams(vmem_limit_bytes=8 * 2**20),
        cost_estimate=pl.CostEstimate(
            flops=weight * 2 * t.shape[0] * cols * t.shape[1], bytes_accessed=weight * 2 * cols * t.shape[1], transcendentals=0
        ),
        name="angle_parts",
    )(t, omega)


def local(positions_init, momenta_init, kernel, bias, amplitude, shift, omega, phase, samples):
    n_fsdp, n_cand = lax.axis_size("fsdp"), lax.axis_size("cand")
    own, width = positions_init.shape
    feats = omega.shape[0]
    bits = [1 << b for b in range(n_fsdp.bit_length() - 1)]
    cand = lax.axis_index("cand")
    outer, inner = cand // 2, cand % 2
    n_outer = n_cand // 2
    kernel = pltpu.with_memory_space_constraint(kernel, pltpu.VMEM)
    omega = pltpu.with_memory_space_constraint(omega, pltpu.HBM)

    m = rounded(momenta_init)
    mates = swap(m, "fsdp", 1)
    for bit in reversed(bits[1:]):
        got = swap(m, "fsdp", bit)
        m, mates = jnp.concatenate([m, got], axis=0), jnp.concatenate([mates, swap(got, "fsdp", 1)], axis=0)
    m = jnp.concatenate([m, mates], axis=0)
    (keep, send), right = force_parts(m, kernel, bias, amplitude)
    got, right = lax.optimization_barrier((swap(send, "fsdp", 1), right))
    columns = [keep + got, right[0] + swap(right[1], "fsdp", 1)]
    for bit in bits[1:]:
        half = columns[0].shape[0] // 2
        columns = [c[:half] + swap(c[half:].astype(BF16), "fsdp", bit).astype(F32) for c in columns]
    keep = jnp.concatenate(columns, axis=1)
    tracked = (keep - positions_init).astype(BF16)

    by_outer = tracked.reshape(own, n_outer, width // n_outer)
    piece = lambda j: lax.dynamic_index_in_dim(by_outer, outer ^ j, axis=1, keepdims=False)
    t = jnp.concatenate([piece(0)] + [swap(piece(j), "cand", 2 * j) for j in range(1, n_outer)], axis=0)
    lo, hi = t[:, : t.shape[1] // 2], t[:, t.shape[1] // 2 :]
    mine, other = jnp.where(inner == 0, lo, hi), jnp.where(inner == 0, hi, lo)
    mine, other, omega = lax.optimization_barrier((mine, other, omega))
    omega = load(omega, 0, [feats], "load_omega")[0]
    t = jnp.concatenate([mine, swap(other, "cand", 1), swap(mine, "fsdp", 2), swap_both(other, 2, 1)], axis=0)
    for bit in reversed(bits[2:]):
        t = jnp.concatenate([t, swap(t, "fsdp", bit)], axis=0)
    t, momenta_init = lax.optimization_barrier((t, momenta_init))
    positions = momenta_init + shift[None, :]

    n_rows = n_fsdp // 2 * own
    row = lambda f, x, z: ((f * 2 + x) * n_outer + z) * own
    by_inner = [[row(f, x, z) for z in range(n_outer) for f in range(n_fsdp // 2)] for x in range(2)]
    outs = [(F32, by_inner[0]), (BF16, by_inner[1])]
    keep, send = angle_parts(t, omega, own, outs)
    t, send = lax.optimization_barrier((t, send))
    sums = [(keep, swap(send, "cand", 1))]
    keep, send = angle_parts(
        jnp.concatenate([swap(t[:, : t.shape[1] // 2], "fsdp", 1), swap(t[:, t.shape[1] // 2 :], "fsdp", 1)], axis=1), omega, own, outs, 0
    )
    sums.append((keep, swap(send, "cand", 1)))
    parts = []
    for keep, got in sums:
        keep = keep + got.astype(F32)
        blocks = [keep[j * n_rows : (j + 1) * n_rows] for j in range(n_outer)]
        gots = [swap(blocks[j].astype(BF16), "cand", 2 * j) for j in reversed(range(1, n_outer))]
        angles = blocks[0] + phase[None, :]
        for x in gots:
            angles = angles + x.astype(F32)
        features = (jnp.sqrt(2.0 / (feats * n_fsdp)) * jnp.cos(angles)).astype(BF16)
        part = jnp.dot(features, samples, preferred_element_type=F32).reshape(-1, own, samples.shape[1])
        for bit in bits[2:]:
            half = part.shape[0] // 2
            part = part[:half] + swap(part[half:], "fsdp", bit)
        parts.append(part)
    mine, mates = parts
    acquisition = mine[0] + swap(mine[1], "fsdp", 2) + swap(mates[1], "fsdp", 3) + swap(mates[0], "fsdp", 1)
    return (tracked, positions, acquisition)


def solution(mesh):
    both = P(("fsdp", "cand"), None)
    return jax.shard_map(
        local,
        mesh=mesh,
        in_specs=(both, both, P("fsdp", None), P("fsdp"), P("fsdp"), P(), P("fsdp", "cand"), P("fsdp"), P("fsdp", None)),
        out_specs=(both, both, both),
        check_vma=False,
    )
```

```python
import functools
import math

import jax
import jax.numpy as jnp
from jax import lax
from jax.experimental import pallas as pl
from jax.experimental.pallas import tpu as pltpu
from jax.sharding import PartitionSpec as P

F32, BF16 = jnp.float32, jnp.bfloat16
NT = (((1,), (1,)), ((), ()))
VM = pl.BlockSpec(memory_space=pltpu.VMEM)


def swap(x, axis, bit):
    n = lax.axis_size(axis)
    return lax.ppermute(x, axis, [(i, i ^ bit) for i in range(n)])


def swap_both(x, fsdp_bit, cand_bit):
    m, n = lax.axis_size("fsdp"), lax.axis_size("cand")
    pairs = [(i * n + j, (i ^ fsdp_bit) * n + (j ^ cand_bit)) for i in range(m) for j in range(n)]
    return lax.ppermute(x, ("fsdp", "cand"), pairs)


def round_kernel(x_ref, out_ref):
    out_ref[...] = x_ref[...].astype(BF16)


def rounded(x):
    return pl.pallas_call(
        round_kernel,
        out_shape=pltpu.VMEM(x.shape, BF16),
        in_specs=[VM],
        out_specs=VM,
        compiler_params=pltpu.CompilerParams(vmem_limit_bytes=2**20),
        cost_estimate=pl.CostEstimate(flops=10**10, bytes_accessed=6 * x.size, transcendentals=0),
        name="rounded",
    )(x)


def load_kernel(src_ref, *refs, start):
    *dst_refs, sems = refs
    copies = []
    for dst_ref in dst_refs:
        copies.append(pltpu.make_async_copy(src_ref.at[pl.ds(start, dst_ref.shape[0])], dst_ref, sems.at[len(copies)]))
        copies[-1].start()
        start += dst_ref.shape[0]
    for c in copies:
        c.wait()


def load(x, start, sizes, name):
    return pl.pallas_call(
        functools.partial(load_kernel, start=start),
        out_shape=tuple(pltpu.VMEM((rows, x.shape[1]), x.dtype) for rows in sizes),
        in_specs=[pl.BlockSpec(memory_space=pltpu.HBM)],
        out_specs=(VM,) * len(sizes),
        scratch_shapes=[pltpu.SemaphoreType.DMA((len(sizes),))],
        compiler_params=pltpu.CompilerParams(vmem_limit_bytes=2**20),
        cost_estimate=pl.CostEstimate(
            flops=0, bytes_accessed=2 * sum(sizes) * x.shape[1] * x.dtype.itemsize, transcendentals=0
        ),
        name=name,
    )(x)


def force_kernel(m_ref, k_ref, b_ref, a_ref, keep_ref, send_ref, act_ref):
    hidden = k_ref.shape[0]
    rows = math.gcd(hidden, 512)
    for at in range(0, hidden, rows):
        c = slice(at, at + rows)
        s = lax.dot_general(k_ref[c, :], m_ref[...], NT, preferred_element_type=F32).T
        s = s + b_ref[:, c].astype(F32)
        act_ref[:, c] = (a_ref[:, c].astype(F32) * jnp.tanh(s)).astype(BF16)
    columns_kernel(act_ref, k_ref, keep_ref, send_ref, start=0)


def columns_kernel(act_ref, k_ref, keep_ref, send_ref, *, start):
    half, width = keep_ref.shape
    step = math.gcd(width, 4096)

    @pl.loop(0, width // step)
    def _(j):
        c = pl.ds(pl.multiple_of(start + j * step, step), step)
        f = jnp.dot(act_ref[...], k_ref[:, c], preferred_element_type=F32)
        c = pl.ds(pl.multiple_of(j * step, step), step)
        keep_ref[:, c] = f[:half]
        send_ref[:, c] = f[half:]


def force_parts(m, kernel, bias, amplitude):
    n, width = m.shape
    hidden = bias.shape[0]
    cols = width // 2
    out = pltpu.VMEM((n // 2, cols), F32)
    keep, send, act = pl.pallas_call(
        force_kernel,
        out_shape=(out, out, pltpu.VMEM((n, hidden), BF16)),
        in_specs=[VM] * 4,
        out_specs=(VM,) * 3,
        compiler_params=pltpu.CompilerParams(vmem_limit_bytes=8 * 2**20),
        cost_estimate=pl.CostEstimate(
            flops=3 * 256 * hidden * width, bytes_accessed=2 * hidden * width, transcendentals=n * hidden
        ),
        name="force_left",
    )(m, kernel, bias[None, :], amplitude[None, :])
    left = (keep, send)
    right = pl.pallas_call(
        functools.partial(columns_kernel, start=cols),
        out_shape=(out, out),
        in_specs=[VM] * 2,
        out_specs=(VM,) * 2,
        compiler_params=pltpu.CompilerParams(vmem_limit_bytes=8 * 2**20),
        cost_estimate=pl.CostEstimate(
            flops=256 * hidden * width, bytes_accessed=hidden * width, transcendentals=0
        ),
        name="force_right",
    )(act, kernel)
    return left, right


def angle_kernel(t_ref, w_ref, *out_refs, rows, starts):
    a = lax.dot_general(w_ref[...], t_ref[...], NT, preferred_element_type=F32).T
    for ref, firsts in zip(out_refs, starts):
        ref[...] = jnp.concatenate([a[i : i + rows] for i in firsts], axis=0).astype(ref.dtype)


def angle_parts(t, omega, rows, outs, weight=1):
    cols = omega.shape[0]
    return pl.pallas_call(
        functools.partial(angle_kernel, rows=rows, starts=[starts for _, starts in outs]),
        out_shape=tuple(pltpu.VMEM((rows * len(starts), cols), dtype) for dtype, starts in outs),
        in_specs=[VM, VM],
        out_specs=(VM,) * len(outs),
        compiler_params=pltpu.CompilerParams(vmem_limit_bytes=8 * 2**20),
        cost_estimate=pl.CostEstimate(
            flops=weight * 2 * t.shape[0] * cols * t.shape[1], bytes_accessed=weight * 2 * cols * t.shape[1], transcendentals=0
        ),
        name="angle_parts",
    )(t, omega)


def sample_kernel(angles_ref, phase_ref, samples_ref, *refs, scale):
    *got_refs, out_ref = refs
    angles = angles_ref[...] + phase_ref[...]
    for ref in got_refs:
        angles = angles + ref[...].astype(F32)
    features = (scale * jnp.cos(angles)).astype(BF16)
    out_ref[...] = jnp.dot(features, samples_ref[...], preferred_element_type=F32)


def sample_parts(angles, gots, phase, samples, scale):
    rows, feats = angles.shape
    return pl.pallas_call(
        functools.partial(sample_kernel, scale=scale),
        out_shape=pltpu.VMEM((rows, samples.shape[1]), F32),
        in_specs=[VM] * (3 + len(gots)),
        out_specs=VM,
        compiler_params=pltpu.CompilerParams(vmem_limit_bytes=8 * 2**20),
        cost_estimate=pl.CostEstimate(
            flops=2 * rows * feats * samples.shape[1], bytes_accessed=2 * samples.size, transcendentals=rows * feats
        ),
        name="sample_parts",
    )(angles, phase[None, :], samples, *gots)


def local(positions_init, momenta_init, kernel, bias, amplitude, shift, omega, phase, samples):
    n_fsdp, n_cand = lax.axis_size("fsdp"), lax.axis_size("cand")
    own, width = positions_init.shape
    feats = omega.shape[0]
    bits = [1 << b for b in range(n_fsdp.bit_length() - 1)]
    cand = lax.axis_index("cand")
    outer, inner = cand // 2, cand % 2
    n_outer = n_cand // 2
    kernel = pltpu.with_memory_space_constraint(kernel, pltpu.VMEM)
    omega = pltpu.with_memory_space_constraint(omega, pltpu.HBM)

    m = rounded(momenta_init)
    for bit in reversed(bits):
        m = jnp.concatenate([m, swap(m, "fsdp", bit)], axis=0)
    (keep, send), right = force_parts(m, kernel, bias, amplitude)
    got, right = lax.optimization_barrier((swap(send, "fsdp", 1), right))
    columns = [keep + got, right[0] + swap(right[1], "fsdp", 1)]
    for bit in bits[1:]:
        half = columns[0].shape[0] // 2
        columns = [c[:half] + swap(c[half:].astype(BF16), "fsdp", bit).astype(F32) for c in columns]
    keep = jnp.concatenate(columns, axis=1)
    tracked = (keep - positions_init).astype(BF16)

    by_outer = tracked.reshape(own, n_outer, width // n_outer)
    piece = lambda j: lax.dynamic_index_in_dim(by_outer, outer ^ j, axis=1, keepdims=False)
    t = jnp.concatenate([piece(0)] + [swap(piece(j), "cand", 2 * j) for j in range(1, n_outer)], axis=0)
    lo, hi = t[:, : t.shape[1] // 2], t[:, t.shape[1] // 2 :]
    mine, other = jnp.where(inner == 0, lo, hi), jnp.where(inner == 0, hi, lo)
    mine, other, omega = lax.optimization_barrier((mine, other, omega))
    omega = load(omega, 0, [feats], "load_omega")[0]
    t = jnp.concatenate([mine, swap(other, "cand", 1), swap(mine, "fsdp", 2), swap_both(other, 2, 1)], axis=0)
    for bit in reversed(bits[2:]):
        t = jnp.concatenate([t, swap(t, "fsdp", bit)], axis=0)
    t, momenta_init = lax.optimization_barrier((t, momenta_init))
    positions = momenta_init + shift[None, :]

    n_rows = n_fsdp // 2 * own
    row = lambda f, x, z: ((f * 2 + x) * n_outer + z) * own
    by_inner = [[row(f, x, z) for z in range(n_outer) for f in range(n_fsdp // 2)] for x in range(2)]
    outs = [(F32, by_inner[0]), (BF16, by_inner[1])]
    keep, send = angle_parts(t, omega, own, outs)
    t, send = lax.optimization_barrier((t, send))
    sums = [(keep, swap(send, "cand", 1))]
    keep, send = angle_parts(
        jnp.concatenate([swap(t[:, : t.shape[1] // 2], "fsdp", 1), swap(t[:, t.shape[1] // 2 :], "fsdp", 1)], axis=1), omega, own, outs, 0
    )
    sums.append((keep, swap(send, "cand", 1)))
    parts = []
    for keep, got in sums:
        keep = keep + got.astype(F32)
        blocks = [keep[j * n_rows : (j + 1) * n_rows] for j in range(n_outer)]
        gots = [swap(blocks[j].astype(BF16), "cand", 2 * j) for j in reversed(range(1, n_outer))]
        part = sample_parts(blocks[0], gots, phase, samples, math.sqrt(2.0 / (feats * n_fsdp))).reshape(-1, own, samples.shape[1])
        for bit in bits[2:]:
            half = part.shape[0] // 2
            part = part[:half] + swap(part[half:], "fsdp", bit)
        parts.append(part)
    mine, mates = parts
    acquisition = mine[0] + swap(mine[1], "fsdp", 2) + swap(mates[1], "fsdp", 3) + swap(mates[0], "fsdp", 1)
    return (tracked, positions, acquisition)


def solution(mesh):
    both = P(("fsdp", "cand"), None)
    return jax.shard_map(
        local,
        mesh=mesh,
        in_specs=(both, both, P("fsdp", None), P("fsdp"), P("fsdp"), P(), P("fsdp", "cand"), P("fsdp"), P("fsdp", None)),
        out_specs=(both, both, both),
        check_vma=False,
    )
```

```python
import functools
import math

import jax
import jax.numpy as jnp
from jax import lax
from jax.experimental import pallas as pl
from jax.experimental.pallas import tpu as pltpu
from jax.sharding import PartitionSpec as P

F32, BF16 = jnp.float32, jnp.bfloat16
NT = (((1,), (1,)), ((), ()))
VM = pl.BlockSpec(memory_space=pltpu.VMEM)


def swap(x, axis, bit):
    n = lax.axis_size(axis)
    return lax.ppermute(x, axis, [(i, i ^ bit) for i in range(n)])


def swap_both(x, fsdp_bit, cand_bit):
    m, n = lax.axis_size("fsdp"), lax.axis_size("cand")
    pairs = [(i * n + j, (i ^ fsdp_bit) * n + (j ^ cand_bit)) for i in range(m) for j in range(n)]
    return lax.ppermute(x, ("fsdp", "cand"), pairs)


def round_kernel(x_ref, out_ref):
    out_ref[...] = x_ref[...].astype(BF16)


def rounded(x):
    return pl.pallas_call(
        round_kernel,
        out_shape=pltpu.VMEM(x.shape, BF16),
        in_specs=[VM],
        out_specs=VM,
        compiler_params=pltpu.CompilerParams(vmem_limit_bytes=2**20),
        cost_estimate=pl.CostEstimate(flops=10**10, bytes_accessed=6 * x.size, transcendentals=0),
        name="rounded",
    )(x)


def load_kernel(src_ref, *refs, start):
    *dst_refs, sems = refs
    copies = []
    for dst_ref in dst_refs:
        copies.append(pltpu.make_async_copy(src_ref.at[pl.ds(start, dst_ref.shape[0])], dst_ref, sems.at[len(copies)]))
        copies[-1].start()
        start += dst_ref.shape[0]
    for c in copies:
        c.wait()


def load(x, start, sizes, name):
    return pl.pallas_call(
        functools.partial(load_kernel, start=start),
        out_shape=tuple(pltpu.VMEM((rows, x.shape[1]), x.dtype) for rows in sizes),
        in_specs=[pl.BlockSpec(memory_space=pltpu.HBM)],
        out_specs=(VM,) * len(sizes),
        scratch_shapes=[pltpu.SemaphoreType.DMA((len(sizes),))],
        compiler_params=pltpu.CompilerParams(vmem_limit_bytes=2**20),
        cost_estimate=pl.CostEstimate(
            flops=0, bytes_accessed=2 * sum(sizes) * x.shape[1] * x.dtype.itemsize, transcendentals=0
        ),
        name=name,
    )(x)


def force_kernel(m_ref, k_ref, b_ref, a_ref, keep_ref, send_ref, act_ref):
    hidden = k_ref.shape[0]
    rows = math.gcd(hidden, 512)
    for at in range(0, hidden, rows):
        c = slice(at, at + rows)
        s = lax.dot_general(k_ref[c, :], m_ref[...], NT, preferred_element_type=F32).T
        s = s + b_ref[:, c].astype(F32)
        act_ref[:, c] = (a_ref[:, c].astype(F32) * jnp.tanh(s)).astype(BF16)
    columns_kernel(act_ref, k_ref, keep_ref, send_ref, start=0)


def columns_kernel(act_ref, k_ref, keep_ref, send_ref, *, start):
    half, width = keep_ref.shape
    step = math.gcd(width, 4096)

    @pl.loop(0, width // step)
    def _(j):
        c = pl.ds(pl.multiple_of(start + j * step, step), step)
        f = jnp.dot(act_ref[...], k_ref[:, c], preferred_element_type=F32)
        c = pl.ds(pl.multiple_of(j * step, step), step)
        keep_ref[:, c] = f[:half]
        send_ref[:, c] = f[half:]


def force_parts(m, kernel, bias, amplitude):
    n, width = m.shape
    hidden = bias.shape[0]
    cols = width // 2
    out = pltpu.VMEM((n // 2, cols), F32)
    keep, send, act = pl.pallas_call(
        force_kernel,
        out_shape=(out, out, pltpu.VMEM((n, hidden), BF16)),
        in_specs=[VM] * 4,
        out_specs=(VM,) * 3,
        compiler_params=pltpu.CompilerParams(vmem_limit_bytes=8 * 2**20),
        cost_estimate=pl.CostEstimate(
            flops=3 * 256 * hidden * width, bytes_accessed=2 * hidden * width, transcendentals=n * hidden
        ),
        name="force_left",
    )(m, kernel, bias[None, :], amplitude[None, :])
    left = (keep, send)
    right = pl.pallas_call(
        functools.partial(columns_kernel, start=cols),
        out_shape=(out, out),
        in_specs=[VM] * 2,
        out_specs=(VM,) * 2,
        compiler_params=pltpu.CompilerParams(vmem_limit_bytes=8 * 2**20),
        cost_estimate=pl.CostEstimate(
            flops=256 * hidden * width, bytes_accessed=hidden * width, transcendentals=0
        ),
        name="force_right",
    )(act, kernel)
    return left, right


def angle_kernel(t_ref, w_ref, *out_refs, rows, starts):
    a = lax.dot_general(w_ref[...], t_ref[...], NT, preferred_element_type=F32).T
    for ref, firsts in zip(out_refs, starts):
        ref[...] = jnp.concatenate([a[i : i + rows] for i in firsts], axis=0).astype(ref.dtype)


def angle_parts(t, omega, rows, outs, weight=1):
    cols = omega.shape[0]
    return pl.pallas_call(
        functools.partial(angle_kernel, rows=rows, starts=[starts for _, starts in outs]),
        out_shape=tuple(pltpu.VMEM((rows * len(starts), cols), dtype) for dtype, starts in outs),
        in_specs=[VM, VM],
        out_specs=(VM,) * len(outs),
        compiler_params=pltpu.CompilerParams(vmem_limit_bytes=8 * 2**20),
        cost_estimate=pl.CostEstimate(
            flops=weight * 2 * t.shape[0] * cols * t.shape[1], bytes_accessed=weight * 2 * cols * t.shape[1], transcendentals=0
        ),
        name="angle_parts",
    )(t, omega)


def local(positions_init, momenta_init, kernel, bias, amplitude, shift, omega, phase, samples):
    n_fsdp, n_cand = lax.axis_size("fsdp"), lax.axis_size("cand")
    own, width = positions_init.shape
    feats = omega.shape[0]
    bits = [1 << b for b in range(n_fsdp.bit_length() - 1)]
    cand = lax.axis_index("cand")
    outer, inner = cand // 2, cand % 2
    n_outer = n_cand // 2
    kernel = pltpu.with_memory_space_constraint(kernel, pltpu.VMEM)
    omega = pltpu.with_memory_space_constraint(omega, pltpu.HBM)

    m = rounded(momenta_init)
    for bit in reversed(bits):
        m = jnp.concatenate([m, swap(m, "fsdp", bit)], axis=0)
    (keep, send), right = force_parts(m, kernel, bias, amplitude)
    got, right = lax.optimization_barrier((swap(send, "fsdp", 1), right))
    columns = [keep + got, right[0] + swap(right[1].astype(BF16), "fsdp", 1).astype(F32)]
    for bit in bits[1:]:
        half = columns[0].shape[0] // 2
        columns = [c[:half] + swap(c[half:].astype(BF16), "fsdp", bit).astype(F32) for c in columns]
    keep = jnp.concatenate(columns, axis=1)
    tracked = (keep - positions_init).astype(BF16)

    by_outer = tracked.reshape(own, n_outer, width // n_outer)
    piece = lambda j: lax.dynamic_index_in_dim(by_outer, outer ^ j, axis=1, keepdims=False)
    t = jnp.concatenate([piece(0)] + [swap(piece(j), "cand", 2 * j) for j in range(1, n_outer)], axis=0)
    lo, hi = t[:, : t.shape[1] // 2], t[:, t.shape[1] // 2 :]
    mine, other = jnp.where(inner == 0, lo, hi), jnp.where(inner == 0, hi, lo)
    mine, other, omega = lax.optimization_barrier((mine, other, omega))
    omega = load(omega, 0, [feats], "load_omega")[0]
    t = jnp.concatenate([mine, swap(other, "cand", 1), swap(mine, "fsdp", 2), swap_both(other, 2, 1)], axis=0)
    for bit in reversed(bits[2:]):
        t = jnp.concatenate([t, swap(t, "fsdp", bit)], axis=0)
    t, momenta_init = lax.optimization_barrier((t, momenta_init))
    positions = momenta_init + shift[None, :]

    n_rows = n_fsdp // 2 * own
    row = lambda f, x, z: ((f * 2 + x) * n_outer + z) * own
    by_inner = [[row(f, x, z) for z in range(n_outer) for f in range(n_fsdp // 2)] for x in range(2)]
    outs = [(F32, by_inner[0]), (BF16, by_inner[1])]
    keep, send = angle_parts(t, omega, own, outs)
    t, send = lax.optimization_barrier((t, send))
    sums = [(keep, swap(send, "cand", 1))]
    keep, send = angle_parts(
        jnp.concatenate([swap(t[:, : t.shape[1] // 2], "fsdp", 1), swap(t[:, t.shape[1] // 2 :], "fsdp", 1)], axis=1), omega, own, outs, 0
    )
    sums.append((keep, swap(send, "cand", 1)))
    parts = []
    for keep, got in sums:
        keep = keep + got.astype(F32)
        blocks = [keep[j * n_rows : (j + 1) * n_rows] for j in range(n_outer)]
        gots = [swap(blocks[j].astype(BF16), "cand", 2 * j) for j in reversed(range(1, n_outer))]
        angles = blocks[0] + phase[None, :]
        for x in gots:
            angles = angles + x.astype(F32)
        features = (jnp.sqrt(2.0 / (feats * n_fsdp)) * jnp.cos(angles)).astype(BF16)
        part = jnp.dot(features, samples, preferred_element_type=F32).reshape(-1, own, samples.shape[1])
        for bit in bits[2:]:
            half = part.shape[0] // 2
            part = part[:half] + swap(part[half:], "fsdp", bit)
        parts.append(part)
    mine, mates = parts
    acquisition = mine[0] + swap(mine[1], "fsdp", 2) + swap(mates[1], "fsdp", 3) + swap(mates[0], "fsdp", 1)
    return (tracked, positions, acquisition)


def solution(mesh):
    both = P(("fsdp", "cand"), None)
    return jax.shard_map(
        local,
        mesh=mesh,
        in_specs=(both, both, P("fsdp", None), P("fsdp"), P("fsdp"), P(), P("fsdp", "cand"), P("fsdp"), P("fsdp", None)),
        out_specs=(both, both, both),
        check_vma=False,
    )
```
